32 devices in a mesh: grp: 2 (over y), blk: 8 (over z, x), pair: 2 (over core).
Axes of the slice: x: 2, y: 2, z: 4, core: 2. Of those that a mesh axis runs over, the one named last changes fastest.
Arguments:
- wavefunc: bfloat16 [96, 16, 2, 768], P(('grp', 'blk')), parts along dimension 0, may hold values from -6 to 6
- haydock: float32 [96, 128], P(('grp', 'blk')), parts along dimension 0, may hold values from -6 to 6
- screened: bfloat16 [16, 768, 768], P(('grp', 'blk')), parts along dimension 0, may hold values from -0.21875 to 0.21875
- coulomb: float32 [1536], P('grp'), parts along dimension 0, may hold values from 0.05 to 1
- umklapp_map: int32 [3, 768], replicated, may hold values from 0 to 767, each once within a row
Outputs:
- kernel_out: float32 [96, 128], P(('grp', 'blk')), parts along dimension 0
The draws below stay inside these ranges and needn't reach their ends.
There are 2 independent parts, one for each index of `grp`. The reference program is written for one: setup_inputs(seed, part) draws one part's arguments, and reference() takes and returns one part's arrays. A program takes and returns all parts, laid end to end along the dimension named above; an argument that names none is the same for every part. Nothing has to cross between parts.
Inputs may be any that keep to these rules, and one draw needn't show every extreme that they name: Each row of umklapp_map is a permutation of 0 .. 767.
All inputs are finite; a program needn't handle non-finite values.
Results may differ from the reference program's by a relative error of at most 0.015.
Values may be sent and summed in bfloat16 or wider, within the bound.
A program may use at most 64 MiB of HBM per device.

```python
import math
import jax
import jax.numpy as jnp
from jax import lax

NV = 8
NC = 8
NG = 768
KR = 6
STOPS = 2
NB = 16
QS = 8
NK = 48
NPSI = 128


def levels(key, extent, cuts, low, largest):
    factor_of, own = 1.0, jax.random.fold_in(key, 6)
    for dim, parts in cuts:
        heights = jnp.exp(jax.random.uniform(jax.random.fold_in(own, dim), (parts,), jnp.float32, low / len(cuts), largest / len(cuts)))
        factor_of = factor_of * jnp.repeat(heights, extent[dim] // parts).reshape([-1 if axis == dim else 1 for axis in range(len(extent))])
    return factor_of


def noise(own_key, dims, spread, limit, pieces=(), kind=jnp.bfloat16):
    factor_of = levels(own_key, dims, pieces, -0.22, 0.18) if pieces else 1.0
    drawn = jax.random.normal(own_key, dims, jnp.float32) * spread * factor_of
    return jnp.minimum(jnp.maximum(drawn, -limit), limit).astype(kind)


def setup_inputs(seed: int = 0, part: int = 0) -> dict:
    keys = jax.random.split(jax.random.key(seed), 6)
    own_keys = jax.random.split(jax.random.fold_in(keys[5], part), 6)
    return {
        "wavefunc": noise(own_keys[0], (NK, NB, 2, NG), 1.0, 6.0, ((0, 8),)),
        "haydock": noise(own_keys[1], (NK, NPSI), 1.0, 6.0, ((0, 8),), jnp.float32),
        "screened": noise(own_keys[2], (QS, NG, NG), NG ** -0.5, 0.21875, ((0, 8),)),
        "coulomb": jnp.clip(jnp.exp(jax.random.uniform(own_keys[3], (NG,), jnp.float32, math.log(0.05), math.log(1.0))), 0.05, 1.0),
        "umklapp_map": jax.vmap(lambda own: jax.random.permutation(own, NG))(jax.random.split(keys[4], (STOPS + 1))).reshape((STOPS + 1, NG)).astype(jnp.int32),
    }


def make_amplitude(wave_rows, amp_rows):
    count = wave_rows.shape[0]
    valence = wave_rows[:, :NV].astype(jnp.float32)
    val_re = valence[:, :, 0]
    val_im = valence[:, :, 1]
    amps = amp_rows.reshape(count, 2, NV, NC)
    amp_re = amps[:, 0]
    amp_im = amps[:, 1]
    out_re = jnp.einsum('kvg,kvc->kcg', val_re, amp_re) - jnp.einsum('kvg,kvc->kcg', val_im, amp_im)
    out_im = jnp.einsum('kvg,kvc->kcg', val_re, amp_im) + jnp.einsum('kvg,kvc->kcg', val_im, amp_re)
    return jnp.stack([out_re, out_im], axis=2).astype(jnp.bfloat16)

def densities(wave_rows):
    wide = wave_rows.astype(jnp.float32)
    val_re = wide[:, :NV, 0][:, :, None, :]
    val_im = wide[:, :NV, 1][:, :, None, :]
    cond_re = wide[:, NV:, 0][:, None, :, :]
    cond_im = wide[:, NV:, 1][:, None, :, :]
    return (val_re * cond_re + val_im * cond_im, val_re * cond_im - val_im * cond_re)

def fold_exchange(dens_re, dens_im, amp_rows):
    count = amp_rows.shape[0]
    amps = amp_rows.reshape(count, 2, NV, NC)
    amp_re = amps[:, 0]
    amp_im = amps[:, 1]
    x_re = jnp.einsum('kvcg,kvc->g', dens_re, amp_re) + jnp.einsum('kvcg,kvc->g', dens_im, amp_im)
    x_im = jnp.einsum('kvcg,kvc->g', dens_re, amp_im) - jnp.einsum('kvcg,kvc->g', dens_im, amp_re)
    return (x_re, x_im)

def exchange_terms(dens_re, dens_im, x_re, x_im, coulomb):
    count = dens_re.shape[0]
    y_re = coulomb * x_re
    y_im = coulomb * x_im
    out_re = jnp.einsum('kvcg,g->kvc', dens_re, y_re) - jnp.einsum('kvcg,g->kvc', dens_im, y_im)
    out_im = jnp.einsum('kvcg,g->kvc', dens_re, y_im) + jnp.einsum('kvcg,g->kvc', dens_im, y_re)
    return jnp.stack([out_re, out_im], axis=1).reshape(count, -1)

def direct_fold(wave_rows, permuted, weight):
    valence = wave_rows[:, :NV].astype(jnp.float32)
    val_re = valence[:, :, 0][:, None, :, None, :]
    val_im = valence[:, :, 1][:, None, :, None, :]
    wide = permuted.astype(jnp.float32)
    ahat_re = wide[:, :NC, 0][None, :, None, :, :]
    ahat_im = wide[:, :NC, 1][None, :, None, :, :]
    cond_re = wide[:, NC:, 0]
    cond_im = wide[:, NC:, 1]
    y_re = val_re * ahat_re + val_im * ahat_im
    y_im = val_re * ahat_im - val_im * ahat_re
    stacked = jnp.stack([y_re, y_im], axis=4).astype(jnp.bfloat16)
    flat = stacked.reshape(-1, weight.shape[1])
    image = jnp.dot(flat, weight.T, preferred_element_type=jnp.float32).reshape(stacked.shape)
    z_re = image[:, :, :, :, 0]
    z_im = image[:, :, :, :, 1]
    e_re = jnp.einsum('kjvcg,jcg->kvg', z_re, cond_re) + jnp.einsum('kjvcg,jcg->kvg', z_im, cond_im)
    e_im = jnp.einsum('kjvcg,jcg->kvg', z_im, cond_re) - jnp.einsum('kjvcg,jcg->kvg', z_re, cond_im)
    return (e_re, e_im)

def finish(wave_rows, e_re, e_im):
    count = wave_rows.shape[0]
    cond = wave_rows[:, NV:].astype(jnp.float32)
    cond_re = cond[:, :, 0]
    cond_im = cond[:, :, 1]
    out_re = jnp.einsum('kcg,kvg->kvc', cond_re, e_re) - jnp.einsum('kcg,kvg->kvc', cond_im, e_im)
    out_im = jnp.einsum('kcg,kvg->kvc', cond_re, e_im) + jnp.einsum('kcg,kvg->kvc', cond_im, e_re)
    return jnp.stack([out_re, out_im], axis=1).reshape(count, -1)

def reference(wavefunc, haydock, screened, coulomb, umklapp_map):
    total = wavefunc.shape[0]
    amplitude = make_amplitude(wavefunc, haydock)
    partner = jnp.concatenate([amplitude, wavefunc[:, NV:]], axis=1)
    dens_re, dens_im = densities(wavefunc)
    x_re, x_im = fold_exchange(dens_re, dens_im, haydock)
    exchange = exchange_terms(dens_re, dens_im, x_re, x_im, coulomb) * (1.0 / (8.0 * math.sqrt(NG * NK)))
    scale_direct = -1.0 / (8.0 * math.sqrt(NG * KR * (STOPS + 1)))

    def per_block(block):
        rows_now = lax.dynamic_slice_in_dim(wavefunc, (block * KR).astype(jnp.int32), KR, 0)
        e_re = jnp.zeros((KR, NV, NG), jnp.float32)
        e_im = jnp.zeros((KR, NV, NG), jnp.float32)
        for stop_index in range(STOPS + 1):
            source = ((block - stop_index) % QS * KR).astype(jnp.int32)
            part_rows = lax.dynamic_slice_in_dim(partner, source, KR, 0)
            permuted = jnp.take(part_rows, umklapp_map[stop_index], axis=3)
            d_re, d_im = direct_fold(rows_now, permuted, screened[stop_index])
            e_re = e_re + d_re
            e_im = e_im + d_im
        return finish(rows_now, e_re, e_im)
    direct = lax.map(per_block, jnp.arange(QS, dtype=jnp.int32))
    direct = direct.reshape(total, -1) * scale_direct
    return direct + exchange
```

```python
import functools
import math

import jax
import jax.numpy as jnp
from jax import lax
from jax.experimental import pallas as pl
from jax.experimental.pallas import tpu as pltpu
from jax.sharding import PartitionSpec as P

NV = 8
NC = 8
STOPS = 2
MESH = pl.DeviceIdType.MESH
NT = (((1,), (1,)), ((), ()))


def dot_nt(a, b):
    return lax.dot_general(a, b, NT, preferred_element_type=jnp.float32)


def dot_nn(a, b):
    return jnp.dot(a, b, preferred_element_type=jnp.float32)


def make_pieces(wave, hay):
    count, bands, _, planes = wave.shape
    rows = wave.reshape(count, 2, NV, 2, planes).transpose(1, 3, 0, 2, 4)
    rows = rows.reshape(2, 2 * count * NV, planes)
    psi = hay.reshape(count, 2, NV, NC).transpose(1, 0, 3, 2)
    eye = jnp.eye(count, dtype=jnp.float32)
    wide = (psi[:, :, :, None, :] * eye[None, :, None, :, None]).reshape(2, count * NC, count * NV)
    top = jnp.concatenate([wide[0], -wide[1]], axis=1)
    low = jnp.concatenate([wide[1], wide[0]], axis=1)
    mix = jnp.concatenate([top, low], axis=0).astype(jnp.bfloat16)
    return rows, mix


def unpack_result(total, count):
    half = count * NC
    out_re = total[:NV, :half] - total[NV:, half : 2 * half]
    out_im = total[NV:, :half] + total[:NV, half : 2 * half]
    out = jnp.stack([out_re, out_im]).reshape(2, NV, count, NC)
    return out.transpose(2, 0, 1, 3).reshape(count, 2 * NV * NC)


def fold_rows(f_rows, cond, count):
    t = dot_nt(f_rows, cond)
    rows, lanes = t.shape
    keep = (lax.broadcasted_iota(jnp.int32, t.shape, 0) // NV) % count == (
        lax.broadcasted_iota(jnp.int32, t.shape, 1) // NC
    ) % count
    t = jnp.where(keep, t, 0.0).reshape(2, count, NV, lanes)
    return jnp.sum(t, axis=1).reshape(2 * NV, lanes)


def kernel(
    count, scale_d, scale_x,
    piece_ref, weight_ref, map_ref, coul_ref, out_ref,
    ubuf, sel, fbuf, stage, res, xbuf,
    recv_near, recv_peer, send_piece, send_res, recv_res, send_x, recv_x,
):
    grp = lax.axis_index("grp")
    me = lax.axis_index("blk")
    p = lax.axis_index("pair")
    blocks = lax.axis_size("blk")
    z = me // 2
    x = me % 2
    worker = me < STOPS + 1
    planes = weight_ref.shape[0]
    half = planes // 2
    edge = count * NV

    barrier = pltpu.get_barrier_semaphore()
    for d in range(1, 2 * blocks):
        other = (me * 2 + p + d) % (2 * blocks)
        pl.semaphore_signal(barrier, inc=1, device_id=(grp, other // 2, other % 2), device_id_type=MESH)
    ubuf[me] = piece_ref[...]
    pl.semaphore_wait(barrier, 2 * blocks - 1)

    def routes(b):
        zb = b // 2
        xb = b % 2
        return (
            (worker & (b != me), me, 1 - p, recv_peer),
            ((z >= 1) & (xb == x) & (zb >= z), me - 2, p, recv_near),
            (((z == 0) & (xb == x)) | ((me == 3) & (xb == 1) & (zb >= 1)), me + 1 - 2 * x, p, recv_near),
            ((me == 0) & (b < 2), me + 2, p, recv_near),
        )

    def copy_of(b, kind, target, core, sems):
        return pltpu.make_async_remote_copy(
            src_ref=ubuf.at[b, p],
            dst_ref=ubuf.at[b, p],
            send_sem=send_piece.at[kind, b],
            recv_sem=sems.at[b],
            device_id=(grp, target, core),
            device_id_type=MESH,
        )

    def forward(b):
        for kind, (go, target, core, sems) in enumerate(routes(b)):
            @pl.when(go)
            def _():
                copy_of(b, kind, target, core, sems).start()

    def drain(b):
        for kind, (go, target, core, sems) in enumerate(routes(b)):
            @pl.when(go)
            def _():
                copy_of(b, kind, target, core, sems).wait_send()

    def arrive(b):
        pltpu.make_async_copy(ubuf.at[b, p], ubuf.at[b, p], recv_near.at[b]).wait()
        forward(b)

    def arrive_peer(b):
        pltpu.make_async_copy(ubuf.at[b, 1 - p], ubuf.at[b, 1 - p], recv_peer.at[b]).wait()

    forward(me)

    cond_own = piece_ref[1, :, :planes].astype(jnp.float32)
    amp = dot_nn(piece_ref[0, :, planes : planes + 2 * edge], piece_ref[0, :, :planes])
    c_re, c_im = cond_own[:edge], cond_own[edge:]
    a_re, a_im = amp[:edge], amp[edge:]
    xbuf[me, 0:1, :] = jnp.sum(c_re * a_re + c_im * a_im, axis=0, keepdims=True)
    xbuf[me, 1:2, :] = jnp.sum(c_re * a_im - c_im * a_re, axis=0, keepdims=True)

    def x_copy(d):
        return pltpu.make_async_remote_copy(
            src_ref=xbuf.at[me],
            dst_ref=xbuf.at[me],
            send_sem=send_x.at[d],
            recv_sem=recv_x.at[me],
            device_id=(grp, (me + d) % blocks, p),
            device_id_type=MESH,
        )

    for d in range(1, blocks):
        x_copy(d).start()

    def res_copy(b, core):
        return pltpu.make_async_remote_copy(
            src_ref=stage.at[b],
            dst_ref=res.at[me * 2 + p],
            send_sem=send_res.at[b, core],
            recv_sem=recv_res.at[me * 2 + p],
            device_id=(grp, b, core),
            device_id_type=MESH,
        )

    @pl.when(worker)
    def _():
        s = me
        base = pl.multiple_of(p * half, 128)
        sel[...] = jnp.where(
            map_ref[...] == lax.broadcasted_iota(jnp.int32, (planes, planes), 1), 1.0, 0.0
        ).astype(jnp.bfloat16)

        def step(t, carry):
            i = jnp.where(s == 2, (t + 2) % blocks, t)
            b = (i + s) % blocks
            first = jnp.where((s == 1) & (t == 0), 0, b)
            take = ((s == 0) & (t >= 1)) | ((s == 1) & (t <= 6)) | ((s == 2) & (t <= 5))
            more = (s == 2) & (t == 1)

            @pl.when(more)
            def _():
                arrive(3)

            @pl.when(take)
            def _():
                arrive(first)
                arrive_peer(first)

            @pl.when(more)
            def _():
                arrive_peer(3)

            val_j = ubuf[i, 0, :, :planes]
            mix_j = ubuf[i, 0, :, planes : planes + 2 * edge]
            amp_j = dot_nn(mix_j, val_j).astype(jnp.bfloat16)
            perm = dot_nt(amp_j, sel[...])
            perm_re = perm.astype(jnp.bfloat16)
            perm_im = jnp.concatenate([perm[edge:], -perm[:edge]], axis=0).astype(jnp.bfloat16)
            cond_t = dot_nt(sel[pl.ds(base, half), :], ubuf[i, 1, :, :planes]).astype(jnp.bfloat16)
            val_b = ubuf[b, 0, :, :planes]
            tile = 128
            for r in range(half // tile):
                rows = pl.ds(pl.multiple_of(base + r * tile, 128), tile)
                w = weight_ref[rows, :].astype(jnp.float32)
                left = cond_t[r * tile : (r + 1) * tile]
                h_re = (dot_nn(left, perm_re) * w).astype(jnp.bfloat16)
                h_im = (dot_nn(left, perm_im) * w).astype(jnp.bfloat16)
                g_re = dot_nt(val_b, h_re)
                g_im = dot_nt(val_b, h_im)
                f_re = g_re[:edge] + g_im[edge:]
                f_im = g_im[:edge] - g_re[edge:]
                fbuf[:, r * tile : (r + 1) * tile] = (
                    jnp.concatenate([f_re, f_im], axis=0) * scale_d
                ).astype(jnp.bfloat16)
            cond_b = ubuf[b, 1, :, pl.ds(base, half)]
            part = fold_rows(fbuf[...], cond_b, count)
            stage[b, :, : 2 * edge] = part
            for core in range(2):
                mine = (b == me) & (p == core)

                @pl.when(mine)
                def _():
                    res[me * 2 + p, :, : 2 * edge] = part

                @pl.when(jnp.logical_not(mine))
                def _():
                    res_copy(b, core).start()

            return carry

        lax.fori_loop(0, blocks, step, 0)

    @pl.when(jnp.logical_not(worker))
    def _():
        for b in range(3, blocks):
            @pl.when((b % 2 == x) & (b // 2 > z))
            def _():
                arrive(b)

    for d in range(1, blocks):
        src = (me + d) % blocks
        pltpu.make_async_copy(xbuf.at[src], xbuf.at[src], recv_x.at[src]).wait()
    y = jnp.sum(xbuf[...], axis=0) * coul_ref[...] * scale_x
    y_re, y_im = y[0:1], y[1:2]
    v_re = piece_ref[0, :edge, :planes].astype(jnp.float32)
    v_im = piece_ref[0, edge:, :planes].astype(jnp.float32)
    f_rows = jnp.concatenate([y_re * v_re + y_im * v_im, y_im * v_re - y_re * v_im], axis=0)
    total = fold_rows(f_rows.astype(jnp.bfloat16), piece_ref[1, :, :planes], count)

    for slot in range(2 * (STOPS + 1)):
        @pl.when(slot != me * 2 + p)
        def _():
            pltpu.make_async_copy(res.at[slot], res.at[slot], recv_res.at[slot]).wait()
    for slot in range(2 * (STOPS + 1)):
        total = total + res[slot, :, : 2 * edge]
    out_ref[...] = total

    for b in range(blocks):
        @pl.when(worker | ((b % 2 == x) & (b // 2 >= z)))
        def _():
            drain(b)
    for d in range(1, blocks):
        x_copy(d).wait_send()

    @pl.when(worker)
    def _():
        for b in range(blocks):
            for core in range(2):
                @pl.when(jnp.logical_not((b == me) & (p == core)))
                def _():
                    res_copy(b, core).wait_send()


def scales(planes, count, total_k):
    return (
        -1.0 / (8.0 * math.sqrt(planes * count * (STOPS + 1))),
        1.0 / (8.0 * math.sqrt(planes * total_k)),
    )


def per_device(wavefunc, haydock, screened, coulomb, umklapp_map):
    count, _, _, planes = wavefunc.shape
    blocks = lax.axis_size("blk")
    edge = count * NV
    rows, mix = make_pieces(wavefunc, haydock)
    mix = jnp.pad(mix, ((0, 0), (0, -2 * edge % 128)))
    pieces = jnp.concatenate([rows, jnp.stack([mix, jnp.zeros_like(mix)])], axis=2)
    stop = jnp.minimum(lax.axis_index("blk"), STOPS)
    index = lax.dynamic_index_in_dim(umklapp_map, stop, 0, keepdims=False).reshape(planes, 1)
    scale_d, scale_x = scales(planes, count, count * blocks)
    lanes = pieces.shape[2]
    vmem = pl.BlockSpec(memory_space=pltpu.VMEM)
    total = pl.pallas_call(
        functools.partial(kernel, count, scale_d, scale_x),
        out_shape=jax.ShapeDtypeStruct((2 * NV, 2 * edge), jnp.float32),
        in_specs=[vmem] * 4,
        out_specs=vmem,
        scratch_shapes=[
            pltpu.VMEM((blocks, 2, 2 * edge, lanes), jnp.bfloat16),
            pltpu.VMEM((planes, planes), jnp.bfloat16),
            pltpu.VMEM((2 * edge, planes // 2), jnp.bfloat16),
            pltpu.VMEM((blocks, 2 * NV, 128), jnp.float32),
            pltpu.VMEM((2 * (STOPS + 1), 2 * NV, 128), jnp.float32),
            pltpu.VMEM((blocks, 2, planes), jnp.float32),
            pltpu.SemaphoreType.DMA((blocks,)),
            pltpu.SemaphoreType.DMA((blocks,)),
            pltpu.SemaphoreType.DMA((4, blocks)),
            pltpu.SemaphoreType.DMA((blocks, 2)),
            pltpu.SemaphoreType.DMA((2 * (STOPS + 1),)),
            pltpu.SemaphoreType.DMA((blocks,)),
            pltpu.SemaphoreType.DMA((blocks,)),
        ],
        compiler_params=pltpu.CompilerParams(
            collective_id=0, has_side_effects=True, vmem_limit_bytes=40 * 1024 * 1024
        ),
    )(pieces, screened[0], index, coulomb.reshape(1, planes))
    return unpack_result(total, count)


def per_device_general(wavefunc, haydock, screened, coulomb, umklapp_map):
    count, _, _, planes = wavefunc.shape
    blocks = lax.axis_size("blk")
    edge = count * NV
    rows, mix = make_pieces(wavefunc, haydock)
    val, cond = rows[0], rows[1]
    amp = dot_nn(mix, val)
    wide = cond.astype(jnp.float32)
    c_re, c_im, a_re, a_im = wide[:edge], wide[edge:], amp[:edge], amp[edge:]
    x_re = jnp.sum(c_re * a_re + c_im * a_im, axis=0)
    x_im = jnp.sum(c_re * a_im - c_im * a_re, axis=0)
    xs = lax.psum(jnp.stack([x_re, x_im]), "blk")
    scale_d, scale_x = scales(planes, count, count * blocks)
    y = xs * coulomb * scale_x
    v_re, v_im = val[:edge].astype(jnp.float32), val[edge:].astype(jnp.float32)
    f = jnp.concatenate([y[0] * v_re + y[1] * v_im, y[1] * v_re - y[0] * v_im], axis=0)
    current = jnp.concatenate([amp.astype(jnp.bfloat16), cond], axis=0)
    for stop in range(STOPS + 1):
        if stop > 0:
            current = lax.ppermute(current, "blk", [(i, (i + 1) % blocks) for i in range(blocks)])
        held = lax.axis_index("blk") == stop
        weight = lax.psum(jnp.where(held, screened[0], jnp.zeros_like(screened[0])), "blk")
        pick = (umklapp_map[stop][:, None] == jnp.arange(planes)[None, :]).astype(jnp.bfloat16)
        perm = dot_nt(current, pick).astype(jnp.bfloat16)
        amp_p, cond_t = perm[: 2 * edge], perm[2 * edge :].T
        turned = jnp.concatenate([amp_p[edge:], -amp_p[:edge]], axis=0)
        h_re = (dot_nn(cond_t, amp_p) * weight.astype(jnp.float32)).astype(jnp.bfloat16)
        h_im = (dot_nn(cond_t, turned) * weight.astype(jnp.float32)).astype(jnp.bfloat16)
        g_re, g_im = dot_nt(val, h_re), dot_nt(val, h_im)
        f = f + scale_d * jnp.concatenate([g_re[:edge] + g_im[edge:], g_im[:edge] - g_re[edge:]], axis=0)
    return unpack_result(fold_rows(f.astype(jnp.bfloat16), cond, count), count)


def solution(mesh):
    placed = (
        P(("grp", "blk"), None, None, None),
        P(("grp", "blk"), None),
        P(("grp", "blk"), None, None),
        P("grp"),
        P(),
    )
    body = per_device if mesh.shape["blk"] == 8 and mesh.shape["pair"] == 2 else per_device_general
    return jax.shard_map(
        body, mesh=mesh, in_specs=placed, out_specs=P(("grp", "blk"), None), check_vma=False
    )
```

```python
import functools
import math

import jax
import jax.numpy as jnp
from jax import lax
from jax.experimental import pallas as pl
from jax.experimental.pallas import tpu as pltpu
from jax.sharding import PartitionSpec as P

NV = 8
NC = 8
STOPS = 2
MESH = pl.DeviceIdType.MESH
NT = (((1,), (1,)), ((), ()))


def dot_nt(a, b):
    return lax.dot_general(a, b, NT, preferred_element_type=jnp.float32)


def dot_nn(a, b):
    return jnp.dot(a, b, preferred_element_type=jnp.float32)


def make_pieces(wave, hay):
    count, bands, _, planes = wave.shape
    rows = wave.reshape(count, 2, NV, 2, planes).transpose(1, 3, 0, 2, 4)
    rows = rows.reshape(2, 2 * count * NV, planes)
    psi = hay.reshape(count, 2, NV, NC).transpose(1, 0, 3, 2)
    eye = jnp.eye(count, dtype=jnp.float32)
    wide = (psi[:, :, :, None, :] * eye[None, :, None, :, None]).reshape(2, count * NC, count * NV)
    top = jnp.concatenate([wide[0], -wide[1]], axis=1)
    low = jnp.concatenate([wide[1], wide[0]], axis=1)
    mix = jnp.concatenate([top, low], axis=0).astype(jnp.bfloat16)
    return rows, mix


def unpack_result(total, count):
    half = count * NC
    out_re = total[:NV, :half] - total[NV:, half : 2 * half]
    out_im = total[NV:, :half] + total[:NV, half : 2 * half]
    out = jnp.stack([out_re, out_im]).reshape(2, NV, count, NC)
    return out.transpose(2, 0, 1, 3).reshape(count, 2 * NV * NC)


def fold_rows(f_rows, cond, count):
    t = dot_nt(f_rows, cond)
    rows, lanes = t.shape
    keep = (lax.broadcasted_iota(jnp.int32, t.shape, 0) // NV) % count == (
        lax.broadcasted_iota(jnp.int32, t.shape, 1) // NC
    ) % count
    t = jnp.where(keep, t, 0.0).reshape(2, count, NV, lanes)
    return jnp.sum(t, axis=1).reshape(2 * NV, lanes)


def kernel(
    count, scale_d, scale_x,
    piece_ref, weight_ref, map_ref, coul_ref, out_ref,
    ubuf, sel, fbuf, stage, res, xbuf,
    recv_near, recv_peer, send_piece, send_res, recv_res, send_x, recv_x,
):
    grp = lax.axis_index("grp")
    me = lax.axis_index("blk")
    p = lax.axis_index("pair")
    blocks = lax.axis_size("blk")
    z = me // 2
    x = me % 2
    worker = me < STOPS + 1
    planes = weight_ref.shape[0]
    half = planes // 2
    edge = count * NV

    barrier = pltpu.get_barrier_semaphore()
    for d in range(1, 2 * blocks):
        other = (me * 2 + p + d) % (2 * blocks)
        pl.semaphore_signal(barrier, inc=1, device_id=(grp, other // 2, other % 2), device_id_type=MESH)
    ubuf[me] = piece_ref[...]
    pl.semaphore_wait(barrier, 2 * blocks - 1)

    def routes(b):
        zb = b // 2
        xb = b % 2
        return (
            (worker & (b != me), me, 1 - p, recv_peer),
            ((b == me) & (me != 0), 0, p, recv_near),
            ((b == me) & (me != 1), 1, p, recv_near),
            ((b == me) & (me != 2), 2, p, recv_near),
        )

    def copy_of(b, kind, target, core, sems):
        return pltpu.make_async_remote_copy(
            src_ref=ubuf.at[b, p],
            dst_ref=ubuf.at[b, p],
            send_sem=send_piece.at[kind, b],
            recv_sem=sems.at[b],
            device_id=(grp, target, core),
            device_id_type=MESH,
        )

    def forward(b):
        for kind, (go, target, core, sems) in enumerate(routes(b)):
            @pl.when(go)
            def _():
                copy_of(b, kind, target, core, sems).start()

    def drain(b):
        for kind, (go, target, core, sems) in enumerate(routes(b)):
            @pl.when(go)
            def _():
                copy_of(b, kind, target, core, sems).wait_send()

    def arrive(b):
        pltpu.make_async_copy(ubuf.at[b, p], ubuf.at[b, p], recv_near.at[b]).wait()
        forward(b)

    def arrive_peer(b):
        pltpu.make_async_copy(ubuf.at[b, 1 - p], ubuf.at[b, 1 - p], recv_peer.at[b]).wait()

    forward(me)

    cond_own = piece_ref[1, :, :planes].astype(jnp.float32)
    amp = dot_nn(piece_ref[0, :, planes : planes + 2 * edge], piece_ref[0, :, :planes])
    c_re, c_im = cond_own[:edge], cond_own[edge:]
    a_re, a_im = amp[:edge], amp[edge:]
    xbuf[me, 0:1, :] = jnp.sum(c_re * a_re + c_im * a_im, axis=0, keepdims=True)
    xbuf[me, 1:2, :] = jnp.sum(c_re * a_im - c_im * a_re, axis=0, keepdims=True)

    def x_copy(d):
        return pltpu.make_async_remote_copy(
            src_ref=xbuf.at[me],
            dst_ref=xbuf.at[me],
            send_sem=send_x.at[d],
            recv_sem=recv_x.at[me],
            device_id=(grp, (me + d) % blocks, p),
            device_id_type=MESH,
        )

    for d in range(1, blocks):
        x_copy(d).start()

    def res_copy(b, core):
        return pltpu.make_async_remote_copy(
            src_ref=stage.at[b],
            dst_ref=res.at[me * 2 + p],
            send_sem=send_res.at[b, core],
            recv_sem=recv_res.at[me * 2 + p],
            device_id=(grp, b, core),
            device_id_type=MESH,
        )

    @pl.when(worker)
    def _():
        s = me
        base = pl.multiple_of(p * half, 128)
        sel[...] = jnp.where(
            map_ref[...] == lax.broadcasted_iota(jnp.int32, (planes, planes), 1), 1.0, 0.0
        ).astype(jnp.bfloat16)

        def step(t, carry):
            i = jnp.where(s == 2, (t + 2) % blocks, t)
            b = (i + s) % blocks
            first = jnp.where((s == 1) & (t == 0), 0, b)
            take = ((s == 0) & (t >= 1)) | ((s == 1) & (t <= 6)) | ((s == 2) & (t <= 5))
            more = (s == 2) & (t == 1)

            @pl.when(more)
            def _():
                arrive(3)

            @pl.when(take)
            def _():
                arrive(first)
                arrive_peer(first)

            @pl.when(more)
            def _():
                arrive_peer(3)

            val_j = ubuf[i, 0, :, :planes]
            mix_j = ubuf[i, 0, :, planes : planes + 2 * edge]
            amp_j = dot_nn(mix_j, val_j).astype(jnp.bfloat16)
            perm = dot_nt(amp_j, sel[...])
            perm_re = perm.astype(jnp.bfloat16)
            perm_im = jnp.concatenate([perm[edge:], -perm[:edge]], axis=0).astype(jnp.bfloat16)
            cond_t = dot_nt(sel[pl.ds(base, half), :], ubuf[i, 1, :, :planes]).astype(jnp.bfloat16)
            val_b = ubuf[b, 0, :, :planes]
            tile = 128
            for r in range(half // tile):
                rows = pl.ds(pl.multiple_of(base + r * tile, 128), tile)
                w = weight_ref[rows, :].astype(jnp.float32)
                left = cond_t[r * tile : (r + 1) * tile]
                h_re = (dot_nn(left, perm_re) * w).astype(jnp.bfloat16)
                h_im = (dot_nn(left, perm_im) * w).astype(jnp.bfloat16)
                g_re = dot_nt(val_b, h_re)
                g_im = dot_nt(val_b, h_im)
                f_re = g_re[:edge] + g_im[edge:]
                f_im = g_im[:edge] - g_re[edge:]
                fbuf[:, r * tile : (r + 1) * tile] = (
                    jnp.concatenate([f_re, f_im], axis=0) * scale_d
                ).astype(jnp.bfloat16)
            cond_b = ubuf[b, 1, :, pl.ds(base, half)]
            part = fold_rows(fbuf[...], cond_b, count)
            stage[b, :, : 2 * edge] = part
            for core in range(2):
                mine = (b == me) & (p == core)

                @pl.when(mine)
                def _():
                    res[me * 2 + p, :, : 2 * edge] = part

                @pl.when(jnp.logical_not(mine))
                def _():
                    res_copy(b, core).start()

            return carry

        lax.fori_loop(0, blocks, step, 0)

    for d in range(1, blocks):
        src = (me + d) % blocks
        pltpu.make_async_copy(xbuf.at[src], xbuf.at[src], recv_x.at[src]).wait()
    y = jnp.sum(xbuf[...], axis=0) * coul_ref[...] * scale_x
    y_re, y_im = y[0:1], y[1:2]
    v_re = piece_ref[0, :edge, :planes].astype(jnp.float32)
    v_im = piece_ref[0, edge:, :planes].astype(jnp.float32)
    f_rows = jnp.concatenate([y_re * v_re + y_im * v_im, y_im * v_re - y_re * v_im], axis=0)
    total = fold_rows(f_rows.astype(jnp.bfloat16), piece_ref[1, :, :planes], count)

    for slot in range(2 * (STOPS + 1)):
        @pl.when(slot != me * 2 + p)
        def _():
            pltpu.make_async_copy(res.at[slot], res.at[slot], recv_res.at[slot]).wait()
    for slot in range(2 * (STOPS + 1)):
        total = total + res[slot, :, : 2 * edge]
    out_ref[...] = total

    for b in range(blocks):
        @pl.when(worker | ((b % 2 == x) & (b // 2 >= z)))
        def _():
            drain(b)
    for d in range(1, blocks):
        x_copy(d).wait_send()

    @pl.when(worker)
    def _():
        for b in range(blocks):
            for core in range(2):
                @pl.when(jnp.logical_not((b == me) & (p == core)))
                def _():
                    res_copy(b, core).wait_send()


def scales(planes, count, total_k):
    return (
        -1.0 / (8.0 * math.sqrt(planes * count * (STOPS + 1))),
        1.0 / (8.0 * math.sqrt(planes * total_k)),
    )


def per_device(wavefunc, haydock, screened, coulomb, umklapp_map):
    count, _, _, planes = wavefunc.shape
    blocks = lax.axis_size("blk")
    edge = count * NV
    rows, mix = make_pieces(wavefunc, haydock)
    mix = jnp.pad(mix, ((0, 0), (0, -2 * edge % 128)))
    pieces = jnp.concatenate([rows, jnp.stack([mix, jnp.zeros_like(mix)])], axis=2)
    stop = jnp.minimum(lax.axis_index("blk"), STOPS)
    index = lax.dynamic_index_in_dim(umklapp_map, stop, 0, keepdims=False).reshape(planes, 1)
    scale_d, scale_x = scales(planes, count, count * blocks)
    lanes = pieces.shape[2]
    vmem = pl.BlockSpec(memory_space=pltpu.VMEM)
    total = pl.pallas_call(
        functools.partial(kernel, count, scale_d, scale_x),
        out_shape=jax.ShapeDtypeStruct((2 * NV, 2 * edge), jnp.float32),
        in_specs=[vmem] * 4,
        out_specs=vmem,
        scratch_shapes=[
            pltpu.VMEM((blocks, 2, 2 * edge, lanes), jnp.bfloat16),
            pltpu.VMEM((planes, planes), jnp.bfloat16),
            pltpu.VMEM((2 * edge, planes // 2), jnp.bfloat16),
            pltpu.VMEM((blocks, 2 * NV, 128), jnp.float32),
            pltpu.VMEM((2 * (STOPS + 1), 2 * NV, 128), jnp.float32),
            pltpu.VMEM((blocks, 2, planes), jnp.float32),
            pltpu.SemaphoreType.DMA((blocks,)),
            pltpu.SemaphoreType.DMA((blocks,)),
            pltpu.SemaphoreType.DMA((4, blocks)),
            pltpu.SemaphoreType.DMA((blocks, 2)),
            pltpu.SemaphoreType.DMA((2 * (STOPS + 1),)),
            pltpu.SemaphoreType.DMA((blocks,)),
            pltpu.SemaphoreType.DMA((blocks,)),
        ],
        compiler_params=pltpu.CompilerParams(
            collective_id=0, has_side_effects=True, vmem_limit_bytes=40 * 1024 * 1024
        ),
    )(pieces, screened[0], index, coulomb.reshape(1, planes))
    return unpack_result(total, count)


def per_device_general(wavefunc, haydock, screened, coulomb, umklapp_map):
    count, _, _, planes = wavefunc.shape
    blocks = lax.axis_size("blk")
    edge = count * NV
    rows, mix = make_pieces(wavefunc, haydock)
    val, cond = rows[0], rows[1]
    amp = dot_nn(mix, val)
    wide = cond.astype(jnp.float32)
    c_re, c_im, a_re, a_im = wide[:edge], wide[edge:], amp[:edge], amp[edge:]
    x_re = jnp.sum(c_re * a_re + c_im * a_im, axis=0)
    x_im = jnp.sum(c_re * a_im - c_im * a_re, axis=0)
    xs = lax.psum(jnp.stack([x_re, x_im]), "blk")
    scale_d, scale_x = scales(planes, count, count * blocks)
    y = xs * coulomb * scale_x
    v_re, v_im = val[:edge].astype(jnp.float32), val[edge:].astype(jnp.float32)
    f = jnp.concatenate([y[0] * v_re + y[1] * v_im, y[1] * v_re - y[0] * v_im], axis=0)
    current = jnp.concatenate([amp.astype(jnp.bfloat16), cond], axis=0)
    for stop in range(STOPS + 1):
        if stop > 0:
            current = lax.ppermute(current, "blk", [(i, (i + 1) % blocks) for i in range(blocks)])
        held = lax.axis_index("blk") == stop
        weight = lax.psum(jnp.where(held, screened[0], jnp.zeros_like(screened[0])), "blk")
        pick = (umklapp_map[stop][:, None] == jnp.arange(planes)[None, :]).astype(jnp.bfloat16)
        perm = dot_nt(current, pick).astype(jnp.bfloat16)
        amp_p, cond_t = perm[: 2 * edge], perm[2 * edge :].T
        turned = jnp.concatenate([amp_p[edge:], -amp_p[:edge]], axis=0)
        h_re = (dot_nn(cond_t, amp_p) * weight.astype(jnp.float32)).astype(jnp.bfloat16)
        h_im = (dot_nn(cond_t, turned) * weight.astype(jnp.float32)).astype(jnp.bfloat16)
        g_re, g_im = dot_nt(val, h_re), dot_nt(val, h_im)
        f = f + scale_d * jnp.concatenate([g_re[:edge] + g_im[edge:], g_im[:edge] - g_re[edge:]], axis=0)
    return unpack_result(fold_rows(f.astype(jnp.bfloat16), cond, count), count)


def solution(mesh):
    placed = (
        P(("grp", "blk"), None, None, None),
        P(("grp", "blk"), None),
        P(("grp", "blk"), None, None),
        P("grp"),
        P(),
    )
    body = per_device if mesh.shape["blk"] == 8 and mesh.shape["pair"] == 2 else per_device_general
    return jax.shard_map(
        body, mesh=mesh, in_specs=placed, out_specs=P(("grp", "blk"), None), check_vma=False
    )
```

```python
import functools
import math

import jax
import jax.numpy as jnp
from jax import lax
from jax.experimental import pallas as pl
from jax.experimental.pallas import tpu as pltpu
from jax.sharding import PartitionSpec as P

NV = 8
NC = 8
STOPS = 2
MESH = pl.DeviceIdType.MESH
NT = (((1,), (1,)), ((), ()))


def dot_nt(a, b):
    return lax.dot_general(a, b, NT, preferred_element_type=jnp.float32)


def dot_nn(a, b):
    return jnp.dot(a, b, preferred_element_type=jnp.float32)


def make_pieces(wave, hay):
    count, bands, _, planes = wave.shape
    rows = wave.reshape(count, 2, NV, 2, planes).transpose(1, 3, 0, 2, 4)
    rows = rows.reshape(2, 2 * count * NV, planes)
    psi = hay.reshape(count, 2, NV, NC).transpose(1, 0, 3, 2)
    eye = jnp.eye(count, dtype=jnp.float32)
    wide = (psi[:, :, :, None, :] * eye[None, :, None, :, None]).reshape(2, count * NC, count * NV)
    top = jnp.concatenate([wide[0], -wide[1]], axis=1)
    low = jnp.concatenate([wide[1], wide[0]], axis=1)
    mix = jnp.concatenate([top, low], axis=0).astype(jnp.bfloat16)
    return rows, mix


def unpack_result(total, count):
    half = count * NC
    out_re = total[:NV, :half] - total[NV:, half : 2 * half]
    out_im = total[NV:, :half] + total[:NV, half : 2 * half]
    out = jnp.stack([out_re, out_im]).reshape(2, NV, count, NC)
    return out.transpose(2, 0, 1, 3).reshape(count, 2 * NV * NC)


def fold_rows(f_rows, cond, count):
    t = dot_nt(f_rows, cond)
    rows, lanes = t.shape
    keep = (lax.broadcasted_iota(jnp.int32, t.shape, 0) // NV) % count == (
        lax.broadcasted_iota(jnp.int32, t.shape, 1) // NC
    ) % count
    t = jnp.where(keep, t, 0.0).reshape(2, count, NV, lanes)
    return jnp.sum(t, axis=1).reshape(2 * NV, lanes)


def kernel(
    count, scale_d, scale_x,
    piece_ref, weight_ref, map_ref, coul_ref, out_ref,
    ubuf, sel, fbuf, stage, res, xbuf,
    recv_near, recv_peer, send_piece, send_res, recv_res, send_x, recv_x,
):
    grp = lax.axis_index("grp")
    me = lax.axis_index("blk")
    p = lax.axis_index("pair")
    blocks = lax.axis_size("blk")
    z = me // 2
    x = me % 2
    worker = me < STOPS + 1
    planes = weight_ref.shape[0]
    half = planes // 2
    edge = count * NV

    barrier = pltpu.get_barrier_semaphore()
    for d in range(1, 2 * blocks):
        other = (me * 2 + p + d) % (2 * blocks)
        pl.semaphore_signal(barrier, inc=1, device_id=(grp, other // 2, other % 2), device_id_type=MESH)
    ubuf[me] = piece_ref[...]
    pl.semaphore_wait(barrier, 2 * blocks - 1)

    def routes(b):
        zb = b // 2
        xb = b % 2
        return (
            (worker & (b != me), me, 1 - p, recv_peer),
            ((b == me) & (me != 0), 0, p, recv_near),
            ((b == me) & (me != 1), 1, p, recv_near),
            ((b == me) & (me != 2), 2, p, recv_near),
        )

    def copy_of(b, kind, target, core, sems):
        return pltpu.make_async_remote_copy(
            src_ref=ubuf.at[b, p],
            dst_ref=ubuf.at[b, p],
            send_sem=send_piece.at[kind, b],
            recv_sem=sems.at[b],
            device_id=(grp, target, core),
            device_id_type=MESH,
        )

    def forward(b):
        for kind, (go, target, core, sems) in enumerate(routes(b)):
            @pl.when(go)
            def _():
                copy_of(b, kind, target, core, sems).start()

    def drain(b):
        for kind, (go, target, core, sems) in enumerate(routes(b)):
            @pl.when(go)
            def _():
                copy_of(b, kind, target, core, sems).wait_send()

    def arrive(b):
        pltpu.make_async_copy(ubuf.at[b, p], ubuf.at[b, p], recv_near.at[b]).wait()
        forward(b)

    def arrive_peer(b):
        pltpu.make_async_copy(ubuf.at[b, 1 - p], ubuf.at[b, 1 - p], recv_peer.at[b]).wait()

    forward(me)

    cond_own = piece_ref[1, :, :planes].astype(jnp.float32)
    amp = dot_nn(piece_ref[0, :, planes : planes + 2 * edge], piece_ref[0, :, :planes])
    c_re, c_im = cond_own[:edge], cond_own[edge:]
    a_re, a_im = amp[:edge], amp[edge:]
    xbuf[me, 0:1, :] = jnp.sum(c_re * a_re + c_im * a_im, axis=0, keepdims=True)
    xbuf[me, 1:2, :] = jnp.sum(c_re * a_im - c_im * a_re, axis=0, keepdims=True)

    def x_copy(d):
        return pltpu.make_async_remote_copy(
            src_ref=xbuf.at[me],
            dst_ref=xbuf.at[me],
            send_sem=send_x.at[d],
            recv_sem=recv_x.at[me],
            device_id=(grp, (me + d) % blocks, p),
            device_id_type=MESH,
        )

    for d in range(1, blocks):
        x_copy(d).start()

    def res_copy(b, core):
        return pltpu.make_async_remote_copy(
            src_ref=stage.at[b],
            dst_ref=res.at[me * 2 + p],
            send_sem=send_res.at[b, core],
            recv_sem=recv_res.at[me * 2 + p],
            device_id=(grp, b, core),
            device_id_type=MESH,
        )

    @pl.when(worker)
    def _():
        s = me
        base = pl.multiple_of(p * half, 128)
        sel[...] = jnp.where(
            map_ref[...] == lax.broadcasted_iota(jnp.int32, (planes, planes), 1), 1.0, 0.0
        ).astype(jnp.bfloat16)

        def step(t, carry):
            i = t
            b = (i + s) % blocks
            first = jnp.where((s >= 1) & (t == 0), 0, jnp.where((s == 2) & (t == 1), 1, b))
            take = ((s == 0) & (t >= 1)) | ((s == 1) & (t <= 6)) | ((s == 2) & (t <= 5))

            @pl.when(t == 0)
            def _():
                for near in range(blocks // 2):
                    @pl.when(near != me)
                    def _():
                        arrive(near)

            @pl.when(take & (first == blocks // 2))
            def _():
                for far in range(blocks // 2, blocks):
                    arrive(far)

            @pl.when(take)
            def _():
                arrive_peer(first)

            @pl.when((s == 2) & (t == 1))
            def _():
                arrive_peer(3)

            val_j = ubuf[i, 0, :, :planes]
            mix_j = ubuf[i, 0, :, planes : planes + 2 * edge]
            amp_j = dot_nn(mix_j, val_j).astype(jnp.bfloat16)
            perm = dot_nt(amp_j, sel[...])
            perm_re = perm.astype(jnp.bfloat16)
            perm_im = jnp.concatenate([perm[edge:], -perm[:edge]], axis=0).astype(jnp.bfloat16)
            cond_t = dot_nt(sel[pl.ds(base, half), :], ubuf[i, 1, :, :planes]).astype(jnp.bfloat16)
            val_b = ubuf[b, 0, :, :planes]
            tile = 128
            for r in range(half // tile):
                rows = pl.ds(pl.multiple_of(base + r * tile, 128), tile)
                w = weight_ref[rows, :].astype(jnp.float32)
                left = cond_t[r * tile : (r + 1) * tile]
                h_re = (dot_nn(left, perm_re) * w).astype(jnp.bfloat16)
                h_im = (dot_nn(left, perm_im) * w).astype(jnp.bfloat16)
                g_re = dot_nt(val_b, h_re)
                g_im = dot_nt(val_b, h_im)
                f_re = g_re[:edge] + g_im[edge:]
                f_im = g_im[:edge] - g_re[edge:]
                fbuf[:, r * tile : (r + 1) * tile] = (
                    jnp.concatenate([f_re, f_im], axis=0) * scale_d
                ).astype(jnp.bfloat16)
            cond_b = ubuf[b, 1, :, pl.ds(base, half)]
            part = fold_rows(fbuf[...], cond_b, count)
            stage[b, :, : 2 * edge] = part
            for core in range(2):
                mine = (b == me) & (p == core)

                @pl.when(mine)
                def _():
                    res[me * 2 + p, :, : 2 * edge] = part

                @pl.when(jnp.logical_not(mine))
                def _():
                    res_copy(b, core).start()

            return carry

        lax.fori_loop(0, blocks, step, 0)

    for d in range(1, blocks):
        src = (me + d) % blocks
        pltpu.make_async_copy(xbuf.at[src], xbuf.at[src], recv_x.at[src]).wait()
    y = jnp.sum(xbuf[...], axis=0) * coul_ref[...] * scale_x
    y_re, y_im = y[0:1], y[1:2]
    v_re = piece_ref[0, :edge, :planes].astype(jnp.float32)
    v_im = piece_ref[0, edge:, :planes].astype(jnp.float32)
    f_rows = jnp.concatenate([y_re * v_re + y_im * v_im, y_im * v_re - y_re * v_im], axis=0)
    total = fold_rows(f_rows.astype(jnp.bfloat16), piece_ref[1, :, :planes], count)

    for slot in range(2 * (STOPS + 1)):
        @pl.when(slot != me * 2 + p)
        def _():
            pltpu.make_async_copy(res.at[slot], res.at[slot], recv_res.at[slot]).wait()
    for slot in range(2 * (STOPS + 1)):
        total = total + res[slot, :, : 2 * edge]
    out_ref[...] = total

    for b in range(blocks):
        @pl.when(worker | ((b % 2 == x) & (b // 2 >= z)))
        def _():
            drain(b)
    for d in range(1, blocks):
        x_copy(d).wait_send()

    @pl.when(worker)
    def _():
        for b in range(blocks):
            for core in range(2):
                @pl.when(jnp.logical_not((b == me) & (p == core)))
                def _():
                    res_copy(b, core).wait_send()


def scales(planes, count, total_k):
    return (
        -1.0 / (8.0 * math.sqrt(planes * count * (STOPS + 1))),
        1.0 / (8.0 * math.sqrt(planes * total_k)),
    )


def per_device(wavefunc, haydock, screened, coulomb, umklapp_map):
    count, _, _, planes = wavefunc.shape
    blocks = lax.axis_size("blk")
    edge = count * NV
    rows, mix = make_pieces(wavefunc, haydock)
    mix = jnp.pad(mix, ((0, 0), (0, -2 * edge % 128)))
    pieces = jnp.concatenate([rows, jnp.stack([mix, jnp.zeros_like(mix)])], axis=2)
    stop = jnp.minimum(lax.axis_index("blk"), STOPS)
    index = lax.dynamic_index_in_dim(umklapp_map, stop, 0, keepdims=False).reshape(planes, 1)
    scale_d, scale_x = scales(planes, count, count * blocks)
    lanes = pieces.shape[2]
    vmem = pl.BlockSpec(memory_space=pltpu.VMEM)
    total = pl.pallas_call(
        functools.partial(kernel, count, scale_d, scale_x),
        out_shape=jax.ShapeDtypeStruct((2 * NV, 2 * edge), jnp.float32),
        in_specs=[vmem] * 4,
        out_specs=vmem,
        scratch_shapes=[
            pltpu.VMEM((blocks, 2, 2 * edge, lanes), jnp.bfloat16),
            pltpu.VMEM((planes, planes), jnp.bfloat16),
            pltpu.VMEM((2 * edge, planes // 2), jnp.bfloat16),
            pltpu.VMEM((blocks, 2 * NV, 128), jnp.float32),
            pltpu.VMEM((2 * (STOPS + 1), 2 * NV, 128), jnp.float32),
            pltpu.VMEM((blocks, 2, planes), jnp.float32),
            pltpu.SemaphoreType.DMA((blocks,)),
            pltpu.SemaphoreType.DMA((blocks,)),
            pltpu.SemaphoreType.DMA((4, blocks)),
            pltpu.SemaphoreType.DMA((blocks, 2)),
            pltpu.SemaphoreType.DMA((2 * (STOPS + 1),)),
            pltpu.SemaphoreType.DMA((blocks,)),
            pltpu.SemaphoreType.DMA((blocks,)),
        ],
        compiler_params=pltpu.CompilerParams(
            collective_id=0, has_side_effects=True, vmem_limit_bytes=40 * 1024 * 1024
        ),
    )(pieces, screened[0], index, coulomb.reshape(1, planes))
    return unpack_result(total, count)


def per_device_general(wavefunc, haydock, screened, coulomb, umklapp_map):
    count, _, _, planes = wavefunc.shape
    blocks = lax.axis_size("blk")
    edge = count * NV
    rows, mix = make_pieces(wavefunc, haydock)
    val, cond = rows[0], rows[1]
    amp = dot_nn(mix, val)
    wide = cond.astype(jnp.float32)
    c_re, c_im, a_re, a_im = wide[:edge], wide[edge:], amp[:edge], amp[edge:]
    x_re = jnp.sum(c_re * a_re + c_im * a_im, axis=0)
    x_im = jnp.sum(c_re * a_im - c_im * a_re, axis=0)
    xs = lax.psum(jnp.stack([x_re, x_im]), "blk")
    scale_d, scale_x = scales(planes, count, count * blocks)
    y = xs * coulomb * scale_x
    v_re, v_im = val[:edge].astype(jnp.float32), val[edge:].astype(jnp.float32)
    f = jnp.concatenate([y[0] * v_re + y[1] * v_im, y[1] * v_re - y[0] * v_im], axis=0)
    current = jnp.concatenate([amp.astype(jnp.bfloat16), cond], axis=0)
    for stop in range(STOPS + 1):
        if stop > 0:
            current = lax.ppermute(current, "blk", [(i, (i + 1) % blocks) for i in range(blocks)])
        held = lax.axis_index("blk") == stop
        weight = lax.psum(jnp.where(held, screened[0], jnp.zeros_like(screened[0])), "blk")
        pick = (umklapp_map[stop][:, None] == jnp.arange(planes)[None, :]).astype(jnp.bfloat16)
        perm = dot_nt(current, pick).astype(jnp.bfloat16)
        amp_p, cond_t = perm[: 2 * edge], perm[2 * edge :].T
        turned = jnp.concatenate([amp_p[edge:], -amp_p[:edge]], axis=0)
        h_re = (dot_nn(cond_t, amp_p) * weight.astype(jnp.float32)).astype(jnp.bfloat16)
        h_im = (dot_nn(cond_t, turned) * weight.astype(jnp.float32)).astype(jnp.bfloat16)
        g_re, g_im = dot_nt(val, h_re), dot_nt(val, h_im)
        f = f + scale_d * jnp.concatenate([g_re[:edge] + g_im[edge:], g_im[:edge] - g_re[edge:]], axis=0)
    return unpack_result(fold_rows(f.astype(jnp.bfloat16), cond, count), count)


def solution(mesh):
    placed = (
        P(("grp", "blk"), None, None, None),
        P(("grp", "blk"), None),
        P(("grp", "blk"), None, None),
        P("grp"),
        P(),
    )
    body = per_device if mesh.shape["blk"] == 8 and mesh.shape["pair"] == 2 else per_device_general
    return jax.shard_map(
        body, mesh=mesh, in_specs=placed, out_specs=P(("grp", "blk"), None), check_vma=False
    )
```

```python
import functools
import math

import jax
import jax.numpy as jnp
from jax import lax
from jax.experimental import pallas as pl
from jax.experimental.pallas import tpu as pltpu
from jax.sharding import PartitionSpec as P

NV = 8
NC = 8
STOPS = 2
MESH = pl.DeviceIdType.MESH
NT = (((1,), (1,)), ((), ()))


def dot_nt(a, b):
    return lax.dot_general(a, b, NT, preferred_element_type=jnp.float32)


def dot_nn(a, b):
    return jnp.dot(a, b, preferred_element_type=jnp.float32)


def make_pieces(wave, hay):
    count, bands, _, planes = wave.shape
    rows = wave.reshape(count, 2, NV, 2, planes).transpose(1, 3, 0, 2, 4)
    rows = rows.reshape(2, 2 * count * NV, planes)
    psi = hay.reshape(count, 2, NV, NC).transpose(1, 0, 3, 2)
    eye = jnp.eye(count, dtype=jnp.float32)
    wide = (psi[:, :, :, None, :] * eye[None, :, None, :, None]).reshape(2, count * NC, count * NV)
    top = jnp.concatenate([wide[0], -wide[1]], axis=1)
    low = jnp.concatenate([wide[1], wide[0]], axis=1)
    mix = jnp.concatenate([top, low], axis=0).astype(jnp.bfloat16)
    return rows, mix


def unpack_result(total, count):
    half = count * NC
    out_re = total[:NV, :half] - total[NV:, half : 2 * half]
    out_im = total[NV:, :half] + total[:NV, half : 2 * half]
    out = jnp.stack([out_re, out_im]).reshape(2, NV, count, NC)
    return out.transpose(2, 0, 1, 3).reshape(count, 2 * NV * NC)


def fold_rows(f_rows, cond, count):
    t = dot_nt(f_rows, cond)
    rows, lanes = t.shape
    keep = (lax.broadcasted_iota(jnp.int32, t.shape, 0) // NV) % count == (
        lax.broadcasted_iota(jnp.int32, t.shape, 1) // NC
    ) % count
    t = jnp.where(keep, t, 0.0).reshape(2, count, NV, lanes)
    return jnp.sum(t, axis=1).reshape(2 * NV, lanes)


def kernel(
    count, scale_d, scale_x,
    piece_ref, weight_ref, map_ref, coul_ref, out_ref,
    ubuf, sel, fbuf, stage, res, xbuf,
    recv_near, recv_peer, send_piece, send_res, recv_res, send_x, recv_x,
):
    grp = lax.axis_index("grp")
    me = lax.axis_index("blk")
    p = lax.axis_index("pair")
    blocks = lax.axis_size("blk")
    z = me // 2
    x = me % 2
    worker = me < STOPS + 1
    planes = weight_ref.shape[0]
    half = planes // 2
    edge = count * NV

    barrier = pltpu.get_barrier_semaphore()
    for d in range(1, 2 * blocks):
        other = (me * 2 + p + d) % (2 * blocks)
        pl.semaphore_signal(barrier, inc=1, device_id=(grp, other // 2, other % 2), device_id_type=MESH)
    ubuf[me] = piece_ref[...]
    pl.semaphore_wait(barrier, 2 * blocks - 1)

    def routes(b):
        zb = b // 2
        xb = b % 2
        return (
            (worker & (b != me), me, 1 - p, recv_peer),
            ((b == me) & (me != 2), 2, p, recv_near),
            ((b == me) & (me != 1), 1, p, recv_near),
            ((b == me) & (me != 0), 0, p, recv_near),
        )

    def copy_of(b, kind, target, core, sems):
        return pltpu.make_async_remote_copy(
            src_ref=ubuf.at[b, p],
            dst_ref=ubuf.at[b, p],
            send_sem=send_piece.at[kind, b],
            recv_sem=sems.at[b],
            device_id=(grp, target, core),
            device_id_type=MESH,
        )

    def forward(b):
        for kind, (go, target, core, sems) in enumerate(routes(b)):
            @pl.when(go)
            def _():
                copy_of(b, kind, target, core, sems).start()

    def drain(b):
        for kind, (go, target, core, sems) in enumerate(routes(b)):
            @pl.when(go)
            def _():
                copy_of(b, kind, target, core, sems).wait_send()

    def arrive(b):
        pltpu.make_async_copy(ubuf.at[b, p], ubuf.at[b, p], recv_near.at[b]).wait()
        forward(b)

    def arrive_peer(b):
        pltpu.make_async_copy(ubuf.at[b, 1 - p], ubuf.at[b, 1 - p], recv_peer.at[b]).wait()

    forward(me)

    cond_own = piece_ref[1, :, :planes].astype(jnp.float32)
    amp = dot_nn(piece_ref[0, :, planes : planes + 2 * edge], piece_ref[0, :, :planes])
    c_re, c_im = cond_own[:edge], cond_own[edge:]
    a_re, a_im = amp[:edge], amp[edge:]
    xbuf[me, 0:1, :] = jnp.sum(c_re * a_re + c_im * a_im, axis=0, keepdims=True)
    xbuf[me, 1:2, :] = jnp.sum(c_re * a_im - c_im * a_re, axis=0, keepdims=True)

    def x_copy(d):
        return pltpu.make_async_remote_copy(
            src_ref=xbuf.at[me],
            dst_ref=xbuf.at[me],
            send_sem=send_x.at[d],
            recv_sem=recv_x.at[me],
            device_id=(grp, (me + d) % blocks, p),
            device_id_type=MESH,
        )

    for d in range(1, blocks):
        x_copy(d).start()

    def res_copy(b, core):
        return pltpu.make_async_remote_copy(
            src_ref=stage.at[b],
            dst_ref=res.at[me * 2 + p],
            send_sem=send_res.at[b, core],
            recv_sem=recv_res.at[me * 2 + p],
            device_id=(grp, b, core),
            device_id_type=MESH,
        )

    @pl.when(worker)
    def _():
        s = me
        base = pl.multiple_of(p * half, 128)
        sel[...] = jnp.where(
            map_ref[...] == lax.broadcasted_iota(jnp.int32, (planes, planes), 1), 1.0, 0.0
        ).astype(jnp.bfloat16)

        def step(t, carry):
            i = t
            b = (i + s) % blocks
            first = jnp.where((s >= 1) & (t == 0), 0, jnp.where((s == 2) & (t == 1), 1, b))
            take = ((s == 0) & (t >= 1)) | ((s == 1) & (t <= 6)) | ((s == 2) & (t <= 5))

            @pl.when(t == 0)
            def _():
                for near in range(blocks // 2):
                    @pl.when(near != me)
                    def _():
                        arrive(near)

            @pl.when(take & (first == blocks // 2))
            def _():
                for far in range(blocks // 2, blocks):
                    arrive(far)

            @pl.when(take)
            def _():
                arrive_peer(first)

            @pl.when((s == 2) & (t == 1))
            def _():
                arrive_peer(3)

            val_j = ubuf[i, 0, :, :planes]
            mix_j = ubuf[i, 0, :, planes : planes + 2 * edge]
            amp_j = dot_nn(mix_j, val_j).astype(jnp.bfloat16)
            perm = dot_nt(amp_j, sel[...])
            perm_re = perm.astype(jnp.bfloat16)
            perm_im = jnp.concatenate([perm[edge:], -perm[:edge]], axis=0).astype(jnp.bfloat16)
            cond_t = dot_nt(sel[pl.ds(base, half), :], ubuf[i, 1, :, :planes]).astype(jnp.bfloat16)
            val_b = ubuf[b, 0, :, :planes]
            tile = 128
            for r in range(half // tile):
                rows = pl.ds(pl.multiple_of(base + r * tile, 128), tile)
                w = weight_ref[rows, :].astype(jnp.float32)
                left = cond_t[r * tile : (r + 1) * tile]
                h_re = (dot_nn(left, perm_re) * w).astype(jnp.bfloat16)
                h_im = (dot_nn(left, perm_im) * w).astype(jnp.bfloat16)
                g_re = dot_nt(val_b, h_re)
                g_im = dot_nt(val_b, h_im)
                f_re = g_re[:edge] + g_im[edge:]
                f_im = g_im[:edge] - g_re[edge:]
                fbuf[:, r * tile : (r + 1) * tile] = (
                    jnp.concatenate([f_re, f_im], axis=0) * scale_d
                ).astype(jnp.bfloat16)
            cond_b = ubuf[b, 1, :, pl.ds(base, half)]
            part = fold_rows(fbuf[...], cond_b, count)
            stage[b, :, : 2 * edge] = part
            for core in range(2):
                mine = (b == me) & (p == core)

                @pl.when(mine)
                def _():
                    res[me * 2 + p, :, : 2 * edge] = part

                @pl.when(jnp.logical_not(mine))
                def _():
                    res_copy(b, core).start()

            return carry

        lax.fori_loop(0, blocks, step, 0)

    for d in range(1, blocks):
        src = (me + d) % blocks
        pltpu.make_async_copy(xbuf.at[src], xbuf.at[src], recv_x.at[src]).wait()
    y = jnp.sum(xbuf[...], axis=0) * coul_ref[...] * scale_x
    y_re, y_im = y[0:1], y[1:2]
    v_re = piece_ref[0, :edge, :planes].astype(jnp.float32)
    v_im = piece_ref[0, edge:, :planes].astype(jnp.float32)
    f_rows = jnp.concatenate([y_re * v_re + y_im * v_im, y_im * v_re - y_re * v_im], axis=0)
    total = fold_rows(f_rows.astype(jnp.bfloat16), piece_ref[1, :, :planes], count)

    for slot in range(2 * (STOPS + 1)):
        @pl.when(slot != me * 2 + p)
        def _():
            pltpu.make_async_copy(res.at[slot], res.at[slot], recv_res.at[slot]).wait()
    for slot in range(2 * (STOPS + 1)):
        total = total + res[slot, :, : 2 * edge]
    out_ref[...] = total

    for b in range(blocks):
        @pl.when(worker | ((b % 2 == x) & (b // 2 >= z)))
        def _():
            drain(b)
    for d in range(1, blocks):
        x_copy(d).wait_send()

    @pl.when(worker)
    def _():
        for b in range(blocks):
            for core in range(2):
                @pl.when(jnp.logical_not((b == me) & (p == core)))
                def _():
                    res_copy(b, core).wait_send()


def scales(planes, count, total_k):
    return (
        -1.0 / (8.0 * math.sqrt(planes * count * (STOPS + 1))),
        1.0 / (8.0 * math.sqrt(planes * total_k)),
    )


def per_device(wavefunc, haydock, screened, coulomb, umklapp_map):
    count, _, _, planes = wavefunc.shape
    blocks = lax.axis_size("blk")
    edge = count * NV
    rows, mix = make_pieces(wavefunc, haydock)
    mix = jnp.pad(mix, ((0, 0), (0, -2 * edge % 128)))
    pieces = jnp.concatenate([rows, jnp.stack([mix, jnp.zeros_like(mix)])], axis=2)
    stop = jnp.minimum(lax.axis_index("blk"), STOPS)
    index = lax.dynamic_index_in_dim(umklapp_map, stop, 0, keepdims=False).reshape(planes, 1)
    scale_d, scale_x = scales(planes, count, count * blocks)
    lanes = pieces.shape[2]
    vmem = pl.BlockSpec(memory_space=pltpu.VMEM)
    total = pl.pallas_call(
        functools.partial(kernel, count, scale_d, scale_x),
        out_shape=jax.ShapeDtypeStruct((2 * NV, 2 * edge), jnp.float32),
        in_specs=[vmem] * 4,
        out_specs=vmem,
        scratch_shapes=[
            pltpu.VMEM((blocks, 2, 2 * edge, lanes), jnp.bfloat16),
            pltpu.VMEM((planes, planes), jnp.bfloat16),
            pltpu.VMEM((2 * edge, planes // 2), jnp.bfloat16),
            pltpu.VMEM((blocks, 2 * NV, 128), jnp.float32),
            pltpu.VMEM((2 * (STOPS + 1), 2 * NV, 128), jnp.float32),
            pltpu.VMEM((blocks, 2, planes), jnp.float32),
            pltpu.SemaphoreType.DMA((blocks,)),
            pltpu.SemaphoreType.DMA((blocks,)),
            pltpu.SemaphoreType.DMA((4, blocks)),
            pltpu.SemaphoreType.DMA((blocks, 2)),
            pltpu.SemaphoreType.DMA((2 * (STOPS + 1),)),
            pltpu.SemaphoreType.DMA((blocks,)),
            pltpu.SemaphoreType.DMA((blocks,)),
        ],
        compiler_params=pltpu.CompilerParams(
            collective_id=0, has_side_effects=True, vmem_limit_bytes=40 * 1024 * 1024
        ),
    )(pieces, screened[0], index, coulomb.reshape(1, planes))
    return unpack_result(total, count)


def per_device_general(wavefunc, haydock, screened, coulomb, umklapp_map):
    count, _, _, planes = wavefunc.shape
    blocks = lax.axis_size("blk")
    edge = count * NV
    rows, mix = make_pieces(wavefunc, haydock)
    val, cond = rows[0], rows[1]
    amp = dot_nn(mix, val)
    wide = cond.astype(jnp.float32)
    c_re, c_im, a_re, a_im = wide[:edge], wide[edge:], amp[:edge], amp[edge:]
    x_re = jnp.sum(c_re * a_re + c_im * a_im, axis=0)
    x_im = jnp.sum(c_re * a_im - c_im * a_re, axis=0)
    xs = lax.psum(jnp.stack([x_re, x_im]), "blk")
    scale_d, scale_x = scales(planes, count, count * blocks)
    y = xs * coulomb * scale_x
    v_re, v_im = val[:edge].astype(jnp.float32), val[edge:].astype(jnp.float32)
    f = jnp.concatenate([y[0] * v_re + y[1] * v_im, y[1] * v_re - y[0] * v_im], axis=0)
    current = jnp.concatenate([amp.astype(jnp.bfloat16), cond], axis=0)
    for stop in range(STOPS + 1):
        if stop > 0:
            current = lax.ppermute(current, "blk", [(i, (i + 1) % blocks) for i in range(blocks)])
        held = lax.axis_index("blk") == stop
        weight = lax.psum(jnp.where(held, screened[0], jnp.zeros_like(screened[0])), "blk")
        pick = (umklapp_map[stop][:, None] == jnp.arange(planes)[None, :]).astype(jnp.bfloat16)
        perm = dot_nt(current, pick).astype(jnp.bfloat16)
        amp_p, cond_t = perm[: 2 * edge], perm[2 * edge :].T
        turned = jnp.concatenate([amp_p[edge:], -amp_p[:edge]], axis=0)
        h_re = (dot_nn(cond_t, amp_p) * weight.astype(jnp.float32)).astype(jnp.bfloat16)
        h_im = (dot_nn(cond_t, turned) * weight.astype(jnp.float32)).astype(jnp.bfloat16)
        g_re, g_im = dot_nt(val, h_re), dot_nt(val, h_im)
        f = f + scale_d * jnp.concatenate([g_re[:edge] + g_im[edge:], g_im[:edge] - g_re[edge:]], axis=0)
    return unpack_result(fold_rows(f.astype(jnp.bfloat16), cond, count), count)


def solution(mesh):
    placed = (
        P(("grp", "blk"), None, None, None),
        P(("grp", "blk"), None),
        P(("grp", "blk"), None, None),
        P("grp"),
        P(),
    )
    body = per_device if mesh.shape["blk"] == 8 and mesh.shape["pair"] == 2 else per_device_general
    return jax.shard_map(
        body, mesh=mesh, in_specs=placed, out_specs=P(("grp", "blk"), None), check_vma=False
    )
```

```python
import functools
import math

import jax
import jax.numpy as jnp
from jax import lax
from jax.experimental import pallas as pl
from jax.experimental.pallas import tpu as pltpu
from jax.sharding import PartitionSpec as P

NV = 8
NC = 8
STOPS = 2
MESH = pl.DeviceIdType.MESH
NT = (((1,), (1,)), ((), ()))


def dot_nt(a, b):
    return lax.dot_general(a, b, NT, preferred_element_type=jnp.float32)


def dot_nn(a, b):
    return jnp.dot(a, b, preferred_element_type=jnp.float32)


def make_pieces(wave, hay):
    count, bands, _, planes = wave.shape
    rows = wave.reshape(count, 2, NV, 2, planes).transpose(1, 3, 0, 2, 4)
    rows = rows.reshape(2, 2 * count * NV, planes)
    psi = hay.reshape(count, 2, NV, NC).transpose(1, 0, 3, 2)
    eye = jnp.eye(count, dtype=jnp.float32)
    wide = (psi[:, :, :, None, :] * eye[None, :, None, :, None]).reshape(2, count * NC, count * NV)
    top = jnp.concatenate([wide[0], -wide[1]], axis=1)
    low = jnp.concatenate([wide[1], wide[0]], axis=1)
    mix = jnp.concatenate([top, low], axis=0).astype(jnp.bfloat16)
    return rows, mix


def unpack_result(total, count):
    half = count * NC
    out_re = total[:NV, :half] - total[NV:, half : 2 * half]
    out_im = total[NV:, :half] + total[:NV, half : 2 * half]
    out = jnp.stack([out_re, out_im]).reshape(2, NV, count, NC)
    return out.transpose(2, 0, 1, 3).reshape(count, 2 * NV * NC)


def fold_rows(f_rows, cond, count):
    t = dot_nt(f_rows, cond)
    rows, lanes = t.shape
    keep = (lax.broadcasted_iota(jnp.int32, t.shape, 0) // NV) % count == (
        lax.broadcasted_iota(jnp.int32, t.shape, 1) // NC
    ) % count
    t = jnp.where(keep, t, 0.0).reshape(2, count, NV, lanes)
    return jnp.sum(t, axis=1).reshape(2 * NV, lanes)


def kernel(
    count, scale_d, scale_x,
    piece_ref, weight_ref, map_ref, coul_ref, out_ref,
    ubuf, sel, fbuf, stage, res, xbuf,
    recv_near, recv_peer, send_piece, send_res, recv_res, send_x, recv_x,
):
    grp = lax.axis_index("grp")
    me = lax.axis_index("blk")
    p = lax.axis_index("pair")
    blocks = lax.axis_size("blk")
    z = me // 2
    x = me % 2
    worker = me < STOPS + 1
    planes = weight_ref.shape[0]
    half = planes // 2
    edge = count * NV

    barrier = pltpu.get_barrier_semaphore()
    for d in range(1, 2 * blocks):
        other = (me * 2 + p + d) % (2 * blocks)
        pl.semaphore_signal(barrier, inc=1, device_id=(grp, other // 2, other % 2), device_id_type=MESH)
    ubuf[me] = piece_ref[...]
    pl.semaphore_wait(barrier, 2 * blocks - 1)

    def routes(b):
        zb = b // 2
        xb = b % 2
        return (
            (worker & (b != me), me, 1 - p, recv_peer),
            ((b == me) & (me != 2), 2, p, recv_near),
            ((b == me) & (me != 1), 1, p, recv_near),
            ((b == me) & (me != 0), 0, p, recv_near),
        )

    widths = (ubuf.shape[3], planes)

    def piece(b, h):
        return ubuf.at[b, h, :, pl.ds(0, widths[h])]

    def copy_of(b, h, kind, target, core, sems):
        return pltpu.make_async_remote_copy(
            src_ref=piece(b, h),
            dst_ref=piece(b, h),
            send_sem=send_piece.at[kind, b],
            recv_sem=sems.at[b],
            device_id=(grp, target, core),
            device_id_type=MESH,
        )

    def forward(b):
        for kind, (go, target, core, sems) in enumerate(routes(b)):
            for h in range(2):
                @pl.when(go & (p == h))
                def _():
                    copy_of(b, h, kind, target, core, sems).start()

    def drain(b):
        for kind, (go, target, core, sems) in enumerate(routes(b)):
            for h in range(2):
                @pl.when(go & (p == h))
                def _():
                    copy_of(b, h, kind, target, core, sems).wait_send()

    def arrive(b):
        for h in range(2):
            @pl.when(p == h)
            def _():
                pltpu.make_async_copy(piece(b, h), piece(b, h), recv_near.at[b]).wait()
        forward(b)

    def arrive_peer(b):
        for h in range(2):
            @pl.when(p == 1 - h)
            def _():
                pltpu.make_async_copy(piece(b, h), piece(b, h), recv_peer.at[b]).wait()

    forward(me)

    cond_own = piece_ref[1, :, :planes].astype(jnp.float32)
    amp = dot_nn(piece_ref[0, :, planes : planes + 2 * edge], piece_ref[0, :, :planes])
    c_re, c_im = cond_own[:edge], cond_own[edge:]
    a_re, a_im = amp[:edge], amp[edge:]
    xbuf[me, 0:1, :] = jnp.sum(c_re * a_re + c_im * a_im, axis=0, keepdims=True)
    xbuf[me, 1:2, :] = jnp.sum(c_re * a_im - c_im * a_re, axis=0, keepdims=True)

    def x_copy(d):
        return pltpu.make_async_remote_copy(
            src_ref=xbuf.at[me],
            dst_ref=xbuf.at[me],
            send_sem=send_x.at[d],
            recv_sem=recv_x.at[me],
            device_id=(grp, (me + d) % blocks, p),
            device_id_type=MESH,
        )

    for d in range(1, blocks):
        x_copy(d).start()

    def res_copy(b, core):
        return pltpu.make_async_remote_copy(
            src_ref=stage.at[b],
            dst_ref=res.at[me * 2 + p],
            send_sem=send_res.at[b, core],
            recv_sem=recv_res.at[me * 2 + p],
            device_id=(grp, b, core),
            device_id_type=MESH,
        )

    @pl.when(worker)
    def _():
        s = me
        base = pl.multiple_of(p * half, 128)
        sel[...] = jnp.where(
            map_ref[...] == lax.broadcasted_iota(jnp.int32, (planes, planes), 1), 1.0, 0.0
        ).astype(jnp.bfloat16)

        def step(t, carry):
            i = t
            b = (i + s) % blocks
            first = jnp.where((s >= 1) & (t == 0), 0, jnp.where((s == 2) & (t == 1), 1, b))
            take = ((s == 0) & (t >= 1)) | ((s == 1) & (t <= 6)) | ((s == 2) & (t <= 5))

            @pl.when(t == 0)
            def _():
                for near in range(blocks // 2):
                    @pl.when(near != me)
                    def _():
                        arrive(near)

            @pl.when(take & (first == blocks // 2))
            def _():
                for far in range(blocks // 2, blocks):
                    arrive(far)

            @pl.when(take)
            def _():
                arrive_peer(first)

            @pl.when((s == 2) & (t == 1))
            def _():
                arrive_peer(3)

            val_j = ubuf[i, 0, :, :planes]
            mix_j = ubuf[i, 0, :, planes : planes + 2 * edge]
            amp_j = dot_nn(mix_j, val_j).astype(jnp.bfloat16)
            perm = dot_nt(amp_j, sel[...])
            perm_re = perm.astype(jnp.bfloat16)
            perm_im = jnp.concatenate([perm[edge:], -perm[:edge]], axis=0).astype(jnp.bfloat16)
            cond_t = dot_nt(sel[pl.ds(base, half), :], ubuf[i, 1, :, :planes]).astype(jnp.bfloat16)
            val_b = ubuf[b, 0, :, :planes]
            tile = 128
            for r in range(half // tile):
                rows = pl.ds(pl.multiple_of(base + r * tile, 128), tile)
                w = weight_ref[rows, :].astype(jnp.float32)
                left = cond_t[r * tile : (r + 1) * tile]
                h_re = (dot_nn(left, perm_re) * w).astype(jnp.bfloat16)
                h_im = (dot_nn(left, perm_im) * w).astype(jnp.bfloat16)
                g_re = dot_nt(val_b, h_re)
                g_im = dot_nt(val_b, h_im)
                f_re = g_re[:edge] + g_im[edge:]
                f_im = g_im[:edge] - g_re[edge:]
                fbuf[:, r * tile : (r + 1) * tile] = (
                    jnp.concatenate([f_re, f_im], axis=0) * scale_d
                ).astype(jnp.bfloat16)
            cond_b = ubuf[b, 1, :, pl.ds(base, half)]
            part = fold_rows(fbuf[...], cond_b, count)
            stage[b, :, : 2 * edge] = part
            for core in range(2):
                mine = (b == me) & (p == core)

                @pl.when(mine)
                def _():
                    res[me * 2 + p, :, : 2 * edge] = part

                @pl.when(jnp.logical_not(mine))
                def _():
                    res_copy(b, core).start()

            return carry

        lax.fori_loop(0, blocks, step, 0)

    for d in range(1, blocks):
        src = (me + d) % blocks
        pltpu.make_async_copy(xbuf.at[src], xbuf.at[src], recv_x.at[src]).wait()
    y = jnp.sum(xbuf[...], axis=0) * coul_ref[...] * scale_x
    y_re, y_im = y[0:1], y[1:2]
    v_re = piece_ref[0, :edge, :planes].astype(jnp.float32)
    v_im = piece_ref[0, edge:, :planes].astype(jnp.float32)
    f_rows = jnp.concatenate([y_re * v_re + y_im * v_im, y_im * v_re - y_re * v_im], axis=0)
    total = fold_rows(f_rows.astype(jnp.bfloat16), piece_ref[1, :, :planes], count)

    for slot in range(2 * (STOPS + 1)):
        @pl.when(slot != me * 2 + p)
        def _():
            pltpu.make_async_copy(res.at[slot], res.at[slot], recv_res.at[slot]).wait()
    for slot in range(2 * (STOPS + 1)):
        total = total + res[slot, :, : 2 * edge]
    out_ref[...] = total

    for b in range(blocks):
        @pl.when(worker | ((b % 2 == x) & (b // 2 >= z)))
        def _():
            drain(b)
    for d in range(1, blocks):
        x_copy(d).wait_send()

    @pl.when(worker)
    def _():
        for b in range(blocks):
            for core in range(2):
                @pl.when(jnp.logical_not((b == me) & (p == core)))
                def _():
                    res_copy(b, core).wait_send()


def scales(planes, count, total_k):
    return (
        -1.0 / (8.0 * math.sqrt(planes * count * (STOPS + 1))),
        1.0 / (8.0 * math.sqrt(planes * total_k)),
    )


def per_device(wavefunc, haydock, screened, coulomb, umklapp_map):
    count, _, _, planes = wavefunc.shape
    blocks = lax.axis_size("blk")
    edge = count * NV
    rows, mix = make_pieces(wavefunc, haydock)
    mix = jnp.pad(mix, ((0, 0), (0, -2 * edge % 128)))
    pieces = jnp.concatenate([rows, jnp.stack([mix, jnp.zeros_like(mix)])], axis=2)
    stop = jnp.minimum(lax.axis_index("blk"), STOPS)
    index = lax.dynamic_index_in_dim(umklapp_map, stop, 0, keepdims=False).reshape(planes, 1)
    scale_d, scale_x = scales(planes, count, count * blocks)
    lanes = pieces.shape[2]
    vmem = pl.BlockSpec(memory_space=pltpu.VMEM)
    total = pl.pallas_call(
        functools.partial(kernel, count, scale_d, scale_x),
        out_shape=jax.ShapeDtypeStruct((2 * NV, 2 * edge), jnp.float32),
        in_specs=[vmem] * 4,
        out_specs=vmem,
        scratch_shapes=[
            pltpu.VMEM((blocks, 2, 2 * edge, lanes), jnp.bfloat16),
            pltpu.VMEM((planes, planes), jnp.bfloat16),
            pltpu.VMEM((2 * edge, planes // 2), jnp.bfloat16),
            pltpu.VMEM((blocks, 2 * NV, 128), jnp.float32),
            pltpu.VMEM((2 * (STOPS + 1), 2 * NV, 128), jnp.float32),
            pltpu.VMEM((blocks, 2, planes), jnp.float32),
            pltpu.SemaphoreType.DMA((blocks,)),
            pltpu.SemaphoreType.DMA((blocks,)),
            pltpu.SemaphoreType.DMA((4, blocks)),
            pltpu.SemaphoreType.DMA((blocks, 2)),
            pltpu.SemaphoreType.DMA((2 * (STOPS + 1),)),
            pltpu.SemaphoreType.DMA((blocks,)),
            pltpu.SemaphoreType.DMA((blocks,)),
        ],
        compiler_params=pltpu.CompilerParams(
            collective_id=0, has_side_effects=True, vmem_limit_bytes=40 * 1024 * 1024
        ),
    )(pieces, screened[0], index, coulomb.reshape(1, planes))
    return unpack_result(total, count)


def per_device_general(wavefunc, haydock, screened, coulomb, umklapp_map):
    count, _, _, planes = wavefunc.shape
    blocks = lax.axis_size("blk")
    edge = count * NV
    rows, mix = make_pieces(wavefunc, haydock)
    val, cond = rows[0], rows[1]
    amp = dot_nn(mix, val)
    wide = cond.astype(jnp.float32)
    c_re, c_im, a_re, a_im = wide[:edge], wide[edge:], amp[:edge], amp[edge:]
    x_re = jnp.sum(c_re * a_re + c_im * a_im, axis=0)
    x_im = jnp.sum(c_re * a_im - c_im * a_re, axis=0)
    xs = lax.psum(jnp.stack([x_re, x_im]), "blk")
    scale_d, scale_x = scales(planes, count, count * blocks)
    y = xs * coulomb * scale_x
    v_re, v_im = val[:edge].astype(jnp.float32), val[edge:].astype(jnp.float32)
    f = jnp.concatenate([y[0] * v_re + y[1] * v_im, y[1] * v_re - y[0] * v_im], axis=0)
    current = jnp.concatenate([amp.astype(jnp.bfloat16), cond], axis=0)
    for stop in range(STOPS + 1):
        if stop > 0:
            current = lax.ppermute(current, "blk", [(i, (i + 1) % blocks) for i in range(blocks)])
        held = lax.axis_index("blk") == stop
        weight = lax.psum(jnp.where(held, screened[0], jnp.zeros_like(screened[0])), "blk")
        pick = (umklapp_map[stop][:, None] == jnp.arange(planes)[None, :]).astype(jnp.bfloat16)
        perm = dot_nt(current, pick).astype(jnp.bfloat16)
        amp_p, cond_t = perm[: 2 * edge], perm[2 * edge :].T
        turned = jnp.concatenate([amp_p[edge:], -amp_p[:edge]], axis=0)
        h_re = (dot_nn(cond_t, amp_p) * weight.astype(jnp.float32)).astype(jnp.bfloat16)
        h_im = (dot_nn(cond_t, turned) * weight.astype(jnp.float32)).astype(jnp.bfloat16)
        g_re, g_im = dot_nt(val, h_re), dot_nt(val, h_im)
        f = f + scale_d * jnp.concatenate([g_re[:edge] + g_im[edge:], g_im[:edge] - g_re[edge:]], axis=0)
    return unpack_result(fold_rows(f.astype(jnp.bfloat16), cond, count), count)


def solution(mesh):
    placed = (
        P(("grp", "blk"), None, None, None),
        P(("grp", "blk"), None),
        P(("grp", "blk"), None, None),
        P("grp"),
        P(),
    )
    body = per_device if mesh.shape["blk"] == 8 and mesh.shape["pair"] == 2 else per_device_general
    return jax.shard_map(
        body, mesh=mesh, in_specs=placed, out_specs=P(("grp", "blk"), None), check_vma=False
    )
```
